256 devices in a mesh: row: 8 (over y, x_hi), col: 32 (over z, x_lo, core).
Axes of the slice: x: 4 (x_hi: 2, x_lo: 2; x = x_hi * 2 + x_lo), y: 4, z: 8, core: 2. Of those that a mesh axis runs over, the one named last changes fastest.
Arguments:
- density: bfloat16 [512, 11, 128, 128], P(('row', 'col')), as said below
- cotangent: bfloat16 [512, 11, 128, 128], P(('row', 'col')), may hold values from -6 to 6
- s_mask: int32 [512, 11], P(('row', 'col')), may hold values from 0 to 1, as said below
- t_mask: int32 [512, 11], P(('row', 'col')), may hold values from 0 to 1, as said below
Outputs:
- purified: float32 [512, 11, 128, 128], P(('row', 'col'))
- gradient: float32 [512, 11, 128, 128], P(('row', 'col'))
The draws below stay inside these ranges and needn't reach their ends.
Inputs may be any that keep to these rules, and one draw needn't show every extreme that they name: `density`: symmetric: entry [i, a] is the transpose of entry [i + a - 5, 10 - a] wherever that row exists. `s_mask`: symmetric in the same sense, one at slot 5, zero where the block column i + a - 5 lies outside the matrix, and every one of it is also one in t_mask. `t_mask`: symmetric in the same sense, one at slot 5, zero where the block column lies outside the matrix.
All inputs are finite; a program needn't handle non-finite values.
Results may differ from the reference program's by a relative error of at most 0.0026.
Values may be sent and summed in bfloat16 or wider, within the bound.
No kernel may reach another device: no remote copies, remote signals or barrier semaphores. Data moves between devices by JAX's collectives and lax.ppermute only.
A program may use at most 384 MiB of HBM per device.

```python
import jax
import jax.numpy as jnp
from jax import lax

BLOCK = 128
HALF = 5
ROWS_DEV = 2
SLOTS = 11
NB = 512


def band_geometry():
    row_index = lax.broadcasted_iota(jnp.int32, (NB, SLOTS), 0)
    slot_index = lax.broadcasted_iota(jnp.int32, (NB, SLOTS), 1)
    partner_row = row_index + slot_index - HALF
    inside = (partner_row >= 0) & (partner_row < NB)
    return (slot_index, jnp.clip(partner_row, 0, NB - 1), SLOTS - 1 - slot_index, inside)


def mask_levels(key):
    levels = jax.random.randint(key, (NB, SLOTS), 0, 16)
    slot_index, partner_row, partner_slot, inside = band_geometry()
    partner = levels[partner_row, partner_slot]
    mirrored = jnp.where(slot_index > HALF, partner, levels)
    return (mirrored, inside, slot_index == HALF)


def draw_t_mask(key, part):
    mirrored, inside, centre = mask_levels(key)
    return jnp.where(inside & ((mirrored < 15) | centre), 1, 0).astype(jnp.int32)


def draw_s_mask(key, part):
    mirrored, inside, centre = mask_levels(key)
    return jnp.where(inside & ((mirrored < 12) | centre), 1, 0).astype(jnp.int32)


def draw_density(key, part):
    key = jax.random.fold_in(key, 11)
    sample = jax.random.normal(key, (NB, SLOTS, BLOCK, BLOCK), jnp.float32)
    slot_index, partner_row, partner_slot, inside = band_geometry()
    flipped = jnp.swapaxes(sample[partner_row, partner_slot], 2, 3)
    slot_wide = slot_index[:, :, None, None]
    centre_part = (sample + jnp.swapaxes(sample, 2, 3)) * 0.70710678
    mirrored = jnp.where(slot_wide < HALF, sample, jnp.where(slot_wide > HALF, flipped, centre_part))
    mirrored = jnp.where(inside[:, :, None, None], mirrored, 0.0)
    scale = 0.8 / jnp.sqrt(0.75 * SLOTS * BLOCK)
    return (mirrored * scale).astype(jnp.bfloat16)


def steps_of(rng, extent, cuts, smallest, high):
    factor_of, own = 1.0, jax.random.fold_in(rng, 6)
    for axis_at, parts in cuts:
        draws = jnp.exp(jax.random.uniform(jax.random.fold_in(own, axis_at), (parts,), jnp.float32, smallest / len(cuts), high / len(cuts)))
        factor_of = factor_of * jnp.repeat(draws, extent[axis_at] // parts).reshape([-1 if axis == axis_at else 1 for axis in range(len(extent))])
    return factor_of


def gaussian(key, dims, spread, most, cuts=(), kind=jnp.bfloat16):
    drawn = spread * jax.random.normal(key, dims, jnp.float32)
    if cuts:
        drawn = drawn * steps_of(key, dims, cuts, -0.22, 0.18)
    return jnp.clip(drawn, -most, most).astype(kind)


def setup_inputs(seed: int = 0) -> dict:
    key_list = jax.random.split(jax.random.key(seed), 5)
    density = draw_density(jax.random.fold_in(key_list[4], 71), 0)
    cotangent = gaussian(key_list[1], (NB, SLOTS, BLOCK, BLOCK), 0.5, 6.0, ((0, 256),))
    s_mask = draw_s_mask(jax.random.fold_in(key_list[4], 71), 0)
    t_mask = draw_t_mask(jax.random.fold_in(key_list[4], 71), 0)
    return dict(density=density, cotangent=cotangent, s_mask=s_mask, t_mask=t_mask)


def band_local(left_side, right_rows):
    row_count = left_side.shape[0]
    slot_count = left_side.shape[1]
    pieces = []
    for offset in range(slot_count):
        shift_by = offset - HALF
        window = right_rows[offset:offset + row_count]
        if shift_by >= 0:
            shifted = jnp.pad(window[:, :slot_count - shift_by], ((0, 0), (shift_by, 0), (0, 0), (0, 0)))
        else:
            shifted = jnp.pad(window[:, -shift_by:], ((0, 0), (0, -shift_by), (0, 0), (0, 0)))
        pieces.append(shifted)
    stacked = jnp.stack(pieces, axis=1).astype(jnp.float32)
    return jnp.einsum("reab,recbd->rcad", left_side.astype(jnp.float32), stacked, precision=lax.Precision.HIGHEST, preferred_element_type=jnp.float32)


def band_product(left_side, right_side):
    padded = jnp.pad(right_side, ((HALF, HALF), (0, 0), (0, 0), (0, 0)))
    group_count = left_side.shape[0] // ROWS_DEV

    def one_group(index):
        start = (index * ROWS_DEV).astype(jnp.int32)
        left_part = lax.dynamic_slice_in_dim(left_side, start, ROWS_DEV, 0)
        right_part = lax.dynamic_slice_in_dim(padded, start, ROWS_DEV + 2 * HALF, 0)
        return band_local(left_part, right_part)

    result = lax.map(one_group, jnp.arange(group_count, dtype=jnp.int32))
    return result.reshape(left_side.shape[0], left_side.shape[1], left_side.shape[2], left_side.shape[3])


def reference(density, cotangent, s_mask, t_mask):
    pattern_keep = s_mask.astype(jnp.float32)[:, :, None, None]
    trunc_keep = t_mask.astype(jnp.float32)[:, :, None, None]
    dense_p = density * s_mask.astype(jnp.bfloat16)[:, :, None, None]
    dense_g = cotangent * t_mask.astype(jnp.bfloat16)[:, :, None, None]
    square = band_product(dense_p, dense_p) * trunc_keep
    square_b = lax.optimization_barrier(square.astype(jnp.bfloat16))
    cubed = band_product(dense_p, square_b) * trunc_keep
    purified = 3.0 * square - 2.0 * cubed
    grad_square = 3.0 * dense_g.astype(jnp.float32) - 2.0 * band_product(dense_p, dense_g) * trunc_keep
    grad_b = lax.optimization_barrier(grad_square.astype(jnp.bfloat16))
    gradient = band_product(grad_b, dense_p) + band_product(dense_p, grad_b) - 2.0 * band_product(dense_g, square_b)
    gradient = gradient * pattern_keep
    return purified, gradient
```

```python
import functools

import jax
import jax.numpy as jnp
from jax import lax
from jax.experimental import pallas as pl
from jax.experimental.pallas import tpu as pltpu
from jax.sharding import PartitionSpec as P

B = 128
HALF = 5
SLOTS = 11
AXES = ("row", "col")
MASK_ROWS = 32
BF16 = jnp.bfloat16
F32 = jnp.float32

NEAR2, FAR2, NEAR4, FAR4, NEAR6 = (1, 2), (3, 4), (5, 6), (7, 8), (9, 10)
P_BLOCKS = {NEAR2: 13, FAR2: 12, NEAR4: 6}
G_PAIRS = (NEAR2, FAR2, NEAR4, FAR4, NEAR6)


def g_blocks(pair):
    return sum(SLOTS - t for t in pair)


def is_near(pair):
    return pair in (NEAR2, NEAR4, NEAR6)


def hop(pair):
    return {NEAR2: 2, FAR2: 2, NEAR4: 4, FAR4: 4, NEAR6: 6}[pair]


def route(pair, devices):
    pairs = []
    for source in range(devices):
        up = (source % 2 == 1) == is_near(pair)
        target = source + hop(pair) if up else source - hop(pair)
        if 0 <= target < devices:
            pairs.append((source, target))
    return pairs


def rows_of(block):
    start = block * B
    if not isinstance(start, int):
        start = pl.multiple_of(start, B)
    return pl.ds(start, B)


def masked(values_ref, mask_ref, row, slot):
    keep = mask_ref[row, slot].astype(F32)
    return (values_ref[row, slot].astype(F32) * keep).astype(BF16)


def pack_density(core_ref, s_ref, t_ref, density_ref, own_ref, near2_ref, far2_ref, near4_ref):
    q = core_ref[0]
    o = 1 - q

    def put(out_ref, at, row, slot):
        out_ref[rows_of(at), :] = masked(density_ref, s_ref, row, slot)

    for s in range(6):
        put(near2_ref, s, q, 5 * o + s)
        put(near2_ref, 6 + s, o, 5 * o + s)
        put(far2_ref, s, o, 5 * q + s)
        put(far2_ref, 6 + s, q, 5 * q + s)
        put(near4_ref, s, q, 5 * o + s)
    put(near2_ref, 12, q, 10 * q)
    for row in range(2):
        for slot in range(SLOTS):
            put(own_ref, row * SLOTS + slot, row, slot)
    line = lax.broadcasted_iota(jnp.int32, (MASK_ROWS, B), 0)
    mask = jnp.zeros((MASK_ROWS, B), F32)
    for row in range(2):
        for slot in range(SLOTS):
            mask = jnp.where(line == row * 16 + slot + 2, t_ref[row, slot].astype(F32), mask)
    mask = mask.astype(BF16)
    for out_ref, count in ((own_ref, 22), (near2_ref, 13), (far2_ref, 12), (near4_ref, 6)):
        out_ref[pl.ds(count * B, MASK_ROWS), :] = mask


def pack_cotangent(core_ref, t_ref, cotangent_ref, own_ref, *out_refs):
    q = core_ref[0]
    o = 1 - q
    for pair, out_ref in zip(G_PAIRS, out_refs):
        up = q if is_near(pair) else o
        at = 0
        for place, t in enumerate(pair):
            row = up if place == 0 else 1 - up
            for s in range(SLOTS - t):
                out_ref[rows_of(at), :] = masked(cotangent_ref, t_ref, row, t * up + s)
                at += 1
    for row in range(2):
        for slot in range(SLOTS):
            own_ref[rows_of(row * SLOTS + slot), :] = masked(cotangent_ref, t_ref, row, slot)


def fetch(copies):
    for copy in copies:
        copy.start()
    for copy in copies:
        copy.wait()


def tile_loop(body):
    for delta in range(-3, 4):
        body_of = functools.partial(body, delta)

        def step(index, carry, body_of=body_of, first=max(0, -delta)):
            body_of(index + first)
            return carry

        lax.fori_loop(0, 6 - abs(delta), step, 0)


def mask_tile(t_ref, first_k, first_j, height):
    rows = []
    for k in range(height):
        pieces = []
        for j in range(2):
            line = (first_k + k) * 16 + (first_j + j) - (first_k + k) + HALF + 2
            pieces.append(jnp.broadcast_to(t_ref[pl.ds(line, 1), :], (B, B)))
        rows.append(jnp.concatenate(pieces, axis=1))
    return jnp.concatenate(rows, axis=0)


def span(j0):
    low = max(0, j0 - 5)
    high = min(11, j0 + 6)
    return low, high - low + 1


NT = (((1,), (1,)), ((), ()))


def square_kernel(
    core_ref, own_p, mate_p, n2_r, n2_x, f2_r, f2_x, n4_r, n4_x, own_g,
    purified_ref, third_ref, pk_ref, t_out_ref,
    row_s, n2_s, f2_s, n4_s, g_s, sw, lhs, t_ref, sems,
):
    p = core_ref[0]
    o = 1 - p
    plan = (
        (own_p, row_s.at[p]), (mate_p, row_s.at[o]),
        (n2_r, n2_s.at[o]), (n2_x, n2_s.at[p]),
        (f2_r, f2_s.at[p]), (f2_x, f2_s.at[o]),
        (n4_r, n4_s.at[o]), (n4_x, n4_s.at[p]),
        (own_g, g_s),
    )
    fetch([pltpu.make_async_copy(a, b, sems.at[i]) for i, (a, b) in enumerate(plan)])

    def held(k, slot):
        if 5 <= k <= 8:
            return row_s[(k - 5) // 2, rows_of(((k - 5) % 2) * SLOTS + slot), :]
        side = 0 if k < 5 else 1
        t = 5 - k if k < 5 else k - 8
        at = slot if k < 5 else slot - 5
        if t <= 2:
            return n2_s[side, rows_of(6 * (t - 1) + at), :]
        if t <= 4:
            return f2_s[side, rows_of(6 * (t - 3) + at), :]
        return n4_s[side, rows_of(at), :]

    def block(k, slot):
        if 5 <= k <= 8 or (k < 5 and slot <= 5) or (k > 8 and slot >= 5):
            return held(k, slot)
        if (k, slot) == (4, 10):
            return n2_s[0, rows_of(12), :]
        if (k, slot) == (9, 0):
            return n2_s[1, rows_of(12), :]
        return held(k + slot - 5, 10 - slot).T

    zero = jnp.zeros((B, B), BF16)
    for pair in range(7):
        for e in range(2):
            rows = pl.ds(e * B, B)
            pk_ref[pair, rows, pl.ds((11 if e == 0 else 0) * B, B)] = zero
            for slot in range(SLOTS):
                pk_ref[pair, rows, pl.ds((slot + e) * B, B)] = block(2 * pair + e, slot)

    for k in range(14):
        if 5 <= k <= 8:
            part = row_s[(k - 5) // 2, pl.ds(22 * B, MASK_ROWS), :]
            r = (k - 5) % 2
        else:
            side = 0 if k < 5 else 1
            t = 5 - k if k < 5 else k - 8
            r = (t % 2) if side == 0 else (1 - t % 2)
            if t <= 2:
                part = n2_s[side, pl.ds(13 * B, MASK_ROWS), :]
            elif t <= 4:
                part = f2_s[side, pl.ds(12 * B, MASK_ROWS), :]
            else:
                part = n4_s[side, pl.ds(6 * B, MASK_ROWS), :]
        t_ref[pl.ds(k * 16, 16), :] = part.astype(F32)[r * 16 : r * 16 + 16, :]
    t_out_ref[...] = t_ref[...]

    for r in range(2):
        hole = pl.ds((11 if r == 0 else 0) * B, B)
        lhs[pl.ds(r * B, B), hole] = zero
        lhs[pl.ds((2 + r) * B, B), hole] = zero
        for slot in range(SLOTS):
            cols = pl.ds((slot + r) * B, B)
            lhs[pl.ds(r * B, B), cols] = row_s[p, rows_of(r * SLOTS + slot), :]
            lhs[pl.ds((2 + r) * B, B), cols] = g_s[rows_of(r * SLOTS + slot), :]

    def tile(delta, j):
        k = j + delta
        count = (12 - 2 * abs(delta)) * B
        left = pk_ref[k + p, :, pl.ds(max(0, -delta) * 2 * B, count)]
        right = pk_ref[j + p, :, pl.ds(max(0, delta) * 2 * B, count)]
        found = lax.dot_general(left, right, NT, preferred_element_type=F32)
        found = found * mask_tile(t_ref, 2 * (k + p), 2 * (j + p), 2)
        sw[pl.ds(pl.multiple_of(k * 256, 256), 256), pl.ds(pl.multiple_of(j * 256, 256), 256)] = (
            found.astype(BF16)
        )

    tile_loop(tile)

    for j in range(6):
        low, count = span(2 * j)
        cols = pl.ds(low * B, count * B)
        right = pk_ref[j + p, :, pl.ds((low + 5 - 2 * j) * B, count * B)]
        square = lax.dot_general(lhs[pl.ds(0, 256), cols], right, NT, preferred_element_type=F32)
        both = jnp.dot(
            lhs[:, cols], sw[pl.ds(low * B, count * B), pl.ds(j * 256, 256)],
            preferred_element_type=F32,
        )
        third_ref[:, pl.ds(j * 256, 256)] = both[256:]
        pure = (3.0 * square - 2.0 * both[:256]) * mask_tile(t_ref, 5 + 2 * p, 2 * j + 2 * p, 2)
        for r in range(2):
            for e in range(2):
                slot = 2 * j + e - r
                if 0 <= slot < SLOTS:
                    purified_ref[r, slot] = pure[r * B : r * B + B, e * B : e * B + B]


def gradient_kernel(
    core_ref, s_ref, own_g, mate_g, n2_r, n2_x, f2_r, f2_x, n4_r, n4_x, f4_r, f4_x, n6_r, n6_x,
    own_p, pk_in, third_in, t_in,
    grad_ref,
    row_s, n2_s, f2_s, n4_s, f4_s, n6_s, own_s, pk_ref, third_s, t_ref, gk, gb, lhs, sems,
):
    p = core_ref[0]
    o = 1 - p
    plan = (
        (own_g, row_s.at[p]), (mate_g, row_s.at[o]),
        (n2_r, n2_s.at[o]), (n2_x, n2_s.at[p]),
        (f2_r, f2_s.at[p]), (f2_x, f2_s.at[o]),
        (n4_r, n4_s.at[o]), (n4_x, n4_s.at[p]),
        (f4_r, f4_s.at[p]), (f4_x, f4_s.at[o]),
        (n6_r, n6_s.at[o]), (n6_x, n6_s.at[p]),
        (own_p, own_s), (t_in, t_ref), (pk_in.at[pl.ds(p, 6)], pk_ref), (third_in, third_s),
    )
    copies = [pltpu.make_async_copy(a, b, sems.at[i]) for i, (a, b) in enumerate(plan)]
    for copy in copies:
        copy.start()
    for copy in copies[:13]:
        copy.wait()

    def block(m, slot):
        if 10 <= m <= 13:
            return row_s[(m - 10) // 2, rows_of(((m - 10) % 2) * SLOTS + slot), :]
        side = 0 if m < 10 else 1
        t = 10 - m if m < 10 else m - 13
        at = slot - t if side == 0 else slot
        store = (n2_s, f2_s, n4_s, f4_s, n6_s)[(t - 1) // 2]
        if t % 2 == 0:
            at += SLOTS - (t - 1)
        return store[side, rows_of(at), :]

    zero = jnp.zeros((B, B), BF16)
    for pair in range(7):
        for e in range(2):
            cols = pl.ds(e * B, B)
            for hole in ((0, 12, 13), (0, 1, 13))[e]:
                gk[pair, pl.ds(hole * B, B), cols] = zero
            j = 2 * pair + e
            for m in range(j, j + 11):
                gk[pair, pl.ds((m - 2 * pair + 1) * B, B), cols] = block(m, j - m + 10)
    for r in range(2):
        lhs[pl.ds(r * B, B), pl.ds((11 if r == 0 else 0) * B, B)] = zero
        for slot in range(SLOTS):
            lhs[pl.ds(r * B, B), pl.ds((slot + r) * B, B)] = own_s[rows_of(r * SLOTS + slot), :]
    for copy in copies[13:]:
        copy.wait()

    def tile(delta, j):
        k = j + delta
        count = (12 - 2 * abs(delta)) * B
        left = pk_ref[k, :, pl.ds(max(0, -delta) * 2 * B, count)]
        right = gk[j + p, pl.ds((max(0, delta) * 2 + 1) * B, count), :]
        found = jnp.dot(left, right, preferred_element_type=F32)
        found = found * mask_tile(t_ref, 2 * (k + p), 2 * (j + p), 2)
        given = gk[j + p, pl.ds((2 * delta + 6) * B, 256), :].astype(F32)
        gb[pl.ds(pl.multiple_of(k * 256, 256), 256), pl.ds(pl.multiple_of(j * 256, 256), 256)] = (
            3.0 * given - 2.0 * found
        ).astype(BF16)

    tile_loop(tile)

    for j in range(6):
        low, count = span(2 * j)
        cols = pl.ds(low * B, count * B)
        right = pk_ref[j, :, pl.ds((low + 5 - 2 * j) * B, count * B)]
        total = lax.dot_general(gb[pl.ds(5 * B, 256), cols], right, NT, preferred_element_type=F32)
        total += jnp.dot(
            lhs[:, cols], gb[pl.ds(low * B, count * B), pl.ds(j * 256, 256)],
            preferred_element_type=F32,
        )
        total -= 2.0 * third_s[:, pl.ds(j * 256, 256)]
        for r in range(2):
            for e in range(2):
                slot = 2 * j + e - r
                if 0 <= slot < SLOTS:
                    keep = s_ref[r, slot].astype(F32)
                    grad_ref[r, slot] = total[r * B : r * B + B, e * B : e * B + B] * keep


SMEM = pl.BlockSpec(memory_space=pltpu.SMEM)
VMEM = pl.BlockSpec(memory_space=pltpu.VMEM)
ANY = pl.BlockSpec(memory_space=pl.ANY)


def flat(blocks, extra=0):
    return jax.ShapeDtypeStruct((blocks * B + extra, B), BF16)


def pair_of(blocks, extra=0):
    return pltpu.VMEM((2, blocks * B + extra, B), BF16)


def on_device(density, cotangent, s_mask, t_mask):
    devices = lax.axis_size(AXES)
    core = (lax.axis_index(AXES) % 2).astype(jnp.int32).reshape(1)
    swap = [(i, i ^ 1) for i in range(devices)]

    def send(message, pair):
        return lax.ppermute(message, AXES, route(pair, devices))

    def to_mate(message):
        return lax.ppermute(message, AXES, swap)

    params = pltpu.CompilerParams(vmem_limit_bytes=48 * 1024 * 1024)
    p_pairs = (NEAR2, FAR2, NEAR4)
    p_out = pl.pallas_call(
        pack_density,
        in_specs=[SMEM, SMEM, SMEM, VMEM],
        out_specs=[VMEM] * 4,
        out_shape=[flat(22, MASK_ROWS)] + [flat(P_BLOCKS[pair], MASK_ROWS) for pair in p_pairs],
        compiler_params=params,
        name="pack_density",
    )(core, s_mask, t_mask, density)
    g_out = pl.pallas_call(
        pack_cotangent,
        in_specs=[SMEM, SMEM, VMEM],
        out_specs=[VMEM] * 6,
        out_shape=[flat(22)] + [flat(g_blocks(pair)) for pair in G_PAIRS],
        compiler_params=params,
        name="pack_cotangent",
    )(core, t_mask, cotangent)
    p_far = [send(message, pair) for message, pair in zip(p_out[1:], p_pairs)]
    mate_p = to_mate(p_out[0])
    mate_g = to_mate(g_out[0])
    p_mate = [to_mate(message) for message in p_far]
    g_far = [send(message, pair) for message, pair in zip(g_out[1:], G_PAIRS)]
    g_mate = [to_mate(message) for message in g_far]

    def zipped(far, mate):
        return [one for both in zip(far, mate) for one in both]

    purified, third, pk, t_all = pl.pallas_call(
        square_kernel,
        in_specs=[SMEM] + [ANY] * 9,
        out_specs=[VMEM] * 4,
        out_shape=[
            jax.ShapeDtypeStruct((2, SLOTS, B, B), F32),
            jax.ShapeDtypeStruct((256, 1536), F32),
            jax.ShapeDtypeStruct((7, 256, 1536), BF16),
            jax.ShapeDtypeStruct((14 * 16, B), F32),
        ],
        scratch_shapes=[
            pair_of(22, MASK_ROWS), pair_of(13, MASK_ROWS), pair_of(12, MASK_ROWS),
            pair_of(6, MASK_ROWS), pltpu.VMEM((22 * B, B), BF16),
            pltpu.VMEM((1536, 1536), BF16), pltpu.VMEM((512, 1536), BF16),
            pltpu.VMEM((14 * 16, B), F32), pltpu.SemaphoreType.DMA((9,)),
        ],
        cost_estimate=pl.CostEstimate(flops=7 * 10**9, bytes_accessed=16 * 10**6, transcendentals=0),
        compiler_params=params,
        name="square",
    )(core, p_out[0], mate_p, *zipped(p_far, p_mate), g_out[0])

    gradient = pl.pallas_call(
        gradient_kernel,
        in_specs=[SMEM, SMEM] + [ANY] * 16,
        out_specs=VMEM,
        out_shape=jax.ShapeDtypeStruct((2, SLOTS, B, B), F32),
        scratch_shapes=[pair_of(22)]
        + [pair_of(g_blocks(pair)) for pair in G_PAIRS]
        + [
            pltpu.VMEM((22 * B + MASK_ROWS, B), BF16), pltpu.VMEM((6, 256, 1536), BF16),
            pltpu.VMEM((256, 1536), F32), pltpu.VMEM((14 * 16, B), F32),
            pltpu.VMEM((7, 14 * B, 256), BF16), pltpu.VMEM((1536, 1536), BF16),
            pltpu.VMEM((256, 1536), BF16), pltpu.SemaphoreType.DMA((16,)),
        ],
        cost_estimate=pl.CostEstimate(flops=7 * 10**9, bytes_accessed=16 * 10**6, transcendentals=0),
        compiler_params=params,
        name="gradient",
    )(core, s_mask, g_out[0], mate_g, *zipped(g_far, g_mate), p_out[0], pk, third, t_all)
    return (purified, gradient)


def solution(mesh):
    band = P(AXES, None, None, None)
    in_specs = (band, band, P(AXES, None), P(AXES, None))
    return jax.shard_map(
        on_device, mesh=mesh, in_specs=in_specs, out_specs=(band, band), check_vma=False
    )
```

```python
import functools

import jax
import jax.numpy as jnp
from jax import lax
from jax.experimental import pallas as pl
from jax.experimental.pallas import tpu as pltpu
from jax.sharding import PartitionSpec as P

B = 128
HALF = 5
SLOTS = 11
AXES = ("row", "col")
MASK_ROWS = 32
BF16 = jnp.bfloat16
F32 = jnp.float32

NEAR2, FAR2, NEAR4, FAR4, NEAR6 = (1, 2), (3, 4), (5, 6), (7, 8), (9, 10)
P_BLOCKS = {NEAR2: 13, FAR2: 12, NEAR4: 6}
G_PAIRS = (NEAR2, FAR2, NEAR4, FAR4, NEAR6)


def g_blocks(pair):
    return sum(SLOTS - t for t in pair)


def is_near(pair):
    return pair in (NEAR2, NEAR4, NEAR6)


def hop(pair):
    return {NEAR2: 2, FAR2: 2, NEAR4: 4, FAR4: 4, NEAR6: 6}[pair]


def route(pair, devices):
    pairs = []
    for source in range(devices):
        up = (source % 2 == 1) == is_near(pair)
        target = source + hop(pair) if up else source - hop(pair)
        if 0 <= target < devices:
            pairs.append((source, target))
    return pairs


def rows_of(block):
    start = block * B
    if not isinstance(start, int):
        start = pl.multiple_of(start, B)
    return pl.ds(start, B)


def masked(values_ref, mask_ref, row, slot):
    keep = mask_ref[row, slot].astype(F32)
    return (values_ref[row, slot].astype(F32) * keep).astype(BF16)


def pack(
    core_ref, s_ref, t_ref, density_any, cotangent_any,
    own_p, near2_ref, far2_ref, near4_ref, own_g, n2_g, f2_g, n4_g, f4_g, n6_g,
    density_ref, cotangent_ref, sems,
):
    first = pltpu.make_async_copy(density_any, density_ref, sems.at[0])
    second = pltpu.make_async_copy(cotangent_any, cotangent_ref, sems.at[1])
    first.start()
    second.start()
    q = core_ref[0]
    o = 1 - q

    line = lax.broadcasted_iota(jnp.int32, (MASK_ROWS, B), 0)
    mask = jnp.zeros((MASK_ROWS, B), F32)
    for row in range(2):
        for slot in range(SLOTS):
            mask = jnp.where(line == row * 16 + slot + 2, t_ref[row, slot].astype(F32), mask)
    mask = mask.astype(BF16)
    for out_ref, count in ((own_p, 22), (near2_ref, 13), (far2_ref, 12), (near4_ref, 6)):
        out_ref[pl.ds(count * B, MASK_ROWS), :] = mask

    first.wait()

    def put(out_ref, at, row, slot):
        out_ref[rows_of(at), :] = masked(density_ref, s_ref, row, slot)

    for s in range(6):
        put(near2_ref, s, q, 5 * o + s)
        put(near2_ref, 6 + s, o, 5 * o + s)
        put(far2_ref, s, o, 5 * q + s)
        put(far2_ref, 6 + s, q, 5 * q + s)
        put(near4_ref, s, q, 5 * o + s)
    put(near2_ref, 12, q, 10 * q)
    for row in range(2):
        for slot in range(SLOTS):
            put(own_p, row * SLOTS + slot, row, slot)

    second.wait()
    for pair, out_ref in zip(G_PAIRS, (n2_g, f2_g, n4_g, f4_g, n6_g)):
        up = q if is_near(pair) else o
        at = 0
        for place, t in enumerate(pair):
            row = up if place == 0 else 1 - up
            for s in range(SLOTS - t):
                out_ref[rows_of(at), :] = masked(cotangent_ref, t_ref, row, t * up + s)
                at += 1
    for row in range(2):
        for slot in range(SLOTS):
            own_g[rows_of(row * SLOTS + slot), :] = masked(cotangent_ref, t_ref, row, slot)


def by_side(core, near, received, other):
    return (other, received) if (core == 0) == near else (received, other)


def in_block(core_ref, work):
    pl.when(core_ref[0] >= 0)(work)


def tile_loop(core_ref, body):
    for delta in range(-3, 4):

        def diagonal(delta=delta):
            for j in range(max(0, -delta), min(6, 6 - delta)):
                body(delta, j)

        in_block(core_ref, diagonal)


def mask_tile(t_ref, first_k, first_j, height):
    rows = []
    for k in range(height):
        pieces = []
        for j in range(2):
            line = (first_k + k) * 16 + (first_j + j) - (first_k + k) + HALF + 2
            pieces.append(jnp.broadcast_to(t_ref[pl.ds(line, 1), :], (B, B)))
        rows.append(jnp.concatenate(pieces, axis=1))
    return jnp.concatenate(rows, axis=0)


def span(j0):
    low = max(0, j0 - 5)
    high = min(11, j0 + 6)
    return low, high - low + 1


NT = (((1,), (1,)), ((), ()))


def square_kernel(
    core_ref, own_p, mate_p, n2_r, n2_x, f2_r, f2_x, n4_r, n4_x, own_g,
    purified_ref, third_ref, pk_ref, t_ref,
    sw, lhs,
):
    p = core_ref[0]
    zero = jnp.zeros((B, B), BF16)

    def assemble(core):
        full = (own_p, mate_p) if core == 0 else (mate_p, own_p)
        n2 = by_side(core, True, n2_r, n2_x)
        f2 = by_side(core, False, f2_r, f2_x)
        n4 = by_side(core, True, n4_r, n4_x)

        def held(k, slot):
            if 5 <= k <= 8:
                return full[(k - 5) // 2][rows_of(((k - 5) % 2) * SLOTS + slot), :]
            side = 0 if k < 5 else 1
            t = 5 - k if k < 5 else k - 8
            at = slot if k < 5 else slot - 5
            if t <= 2:
                return n2[side][rows_of(6 * (t - 1) + at), :]
            if t <= 4:
                return f2[side][rows_of(6 * (t - 3) + at), :]
            return n4[side][rows_of(at), :]

        def block(k, slot):
            if 5 <= k <= 8 or (k < 5 and slot <= 5) or (k > 8 and slot >= 5):
                return held(k, slot)
            if (k, slot) == (4, 10):
                return n2[0][rows_of(12), :]
            if (k, slot) == (9, 0):
                return n2[1][rows_of(12), :]
            return held(k + slot - 5, 10 - slot).T

        for pair in range(core, core + 6):
            for e in range(2):
                rows = pl.ds(e * B, B)
                pk_ref[pair, rows, pl.ds((11 if e == 0 else 0) * B, B)] = zero
                for slot in range(SLOTS):
                    pk_ref[pair, rows, pl.ds((slot + e) * B, B)] = block(2 * pair + e, slot)

        for k in range(14):
            if 5 <= k <= 8:
                part = full[(k - 5) // 2][pl.ds(22 * B, MASK_ROWS), :]
                r = (k - 5) % 2
            else:
                side = 0 if k < 5 else 1
                t = 5 - k if k < 5 else k - 8
                r = (t % 2) if side == 0 else (1 - t % 2)
                if t <= 2:
                    part = n2[side][pl.ds(13 * B, MASK_ROWS), :]
                elif t <= 4:
                    part = f2[side][pl.ds(12 * B, MASK_ROWS), :]
                else:
                    part = n4[side][pl.ds(6 * B, MASK_ROWS), :]
            t_ref[pl.ds(k * 16, 16), :] = part.astype(F32)[r * 16 : r * 16 + 16, :]

    for core in range(2):
        pl.when(p == core)(functools.partial(assemble, core))

    for r in range(2):
        hole = pl.ds((11 if r == 0 else 0) * B, B)
        lhs[pl.ds(r * B, B), hole] = zero
        lhs[pl.ds((2 + r) * B, B), hole] = zero
        for slot in range(SLOTS):
            cols = pl.ds((slot + r) * B, B)
            lhs[pl.ds(r * B, B), cols] = own_p[rows_of(r * SLOTS + slot), :]
            lhs[pl.ds((2 + r) * B, B), cols] = own_g[rows_of(r * SLOTS + slot), :]

    def tile(delta, j):
        k = j + delta
        count = (12 - 2 * abs(delta)) * B
        left = pk_ref[k + p, :, pl.ds(max(0, -delta) * 2 * B, count)]
        right = pk_ref[j + p, :, pl.ds(max(0, delta) * 2 * B, count)]
        found = lax.dot_general(left, right, NT, preferred_element_type=F32)
        found = found * mask_tile(t_ref, 2 * (k + p), 2 * (j + p), 2)
        sw[pl.ds(pl.multiple_of(k * 256, 256), 256), pl.ds(pl.multiple_of(j * 256, 256), 256)] = (
            found.astype(BF16)
        )

    tile_loop(core_ref, tile)

    def finish(j):
        low, count = span(2 * j)
        cols = pl.ds(low * B, count * B)
        right = pk_ref[j + p, :, pl.ds((low + 5 - 2 * j) * B, count * B)]
        square = lax.dot_general(lhs[pl.ds(0, 256), cols], right, NT, preferred_element_type=F32)
        both = jnp.dot(
            lhs[:, cols], sw[pl.ds(low * B, count * B), pl.ds(j * 256, 256)],
            preferred_element_type=F32,
        )
        third_ref[:, pl.ds(j * 256, 256)] = both[256:]
        pure = (3.0 * square - 2.0 * both[:256]) * mask_tile(t_ref, 5 + 2 * p, 2 * j + 2 * p, 2)
        for r in range(2):
            for e in range(2):
                slot = 2 * j + e - r
                if 0 <= slot < SLOTS:
                    purified_ref[r, slot] = pure[r * B : r * B + B, e * B : e * B + B]

    for j in range(6):
        in_block(core_ref, functools.partial(finish, j))


def gradient_kernel(
    core_ref, s_ref, own_g, mate_g, n2_r, n2_x, f2_r, f2_x, n4_r, n4_x, f4_r, f4_x, n6_r, n6_x,
    own_p, pk_ref, third_s, t_ref,
    grad_ref,
    gk, gb, lhs,
):
    p = core_ref[0]
    zero = jnp.zeros((B, B), BF16)

    def assemble(core):
        full = (own_g, mate_g) if core == 0 else (mate_g, own_g)
        stores = (
            by_side(core, True, n2_r, n2_x), by_side(core, False, f2_r, f2_x),
            by_side(core, True, n4_r, n4_x), by_side(core, False, f4_r, f4_x),
            by_side(core, True, n6_r, n6_x),
        )

        def block(m, slot):
            if 10 <= m <= 13:
                return full[(m - 10) // 2][rows_of(((m - 10) % 2) * SLOTS + slot), :]
            side = 0 if m < 10 else 1
            t = 10 - m if m < 10 else m - 13
            at = slot - t if side == 0 else slot
            if t % 2 == 0:
                at += SLOTS - (t - 1)
            return stores[(t - 1) // 2][side][rows_of(at), :]

        for pair in range(core, core + 6):
            for e in range(2):
                cols = pl.ds(e * B, B)
                for hole in ((0, 12, 13), (0, 1, 13))[e]:
                    gk[pair, pl.ds(hole * B, B), cols] = zero
                j = 2 * pair + e
                for m in range(j, j + 11):
                    gk[pair, pl.ds((m - 2 * pair + 1) * B, B), cols] = block(m, j - m + 10)

    for core in range(2):
        pl.when(p == core)(functools.partial(assemble, core))

    for r in range(2):
        lhs[pl.ds(r * B, B), pl.ds((11 if r == 0 else 0) * B, B)] = zero
        for slot in range(SLOTS):
            lhs[pl.ds(r * B, B), pl.ds((slot + r) * B, B)] = own_p[rows_of(r * SLOTS + slot), :]

    def tile(delta, j):
        k = j + delta
        count = (12 - 2 * abs(delta)) * B
        left = pk_ref[k + p, :, pl.ds(max(0, -delta) * 2 * B, count)]
        right = gk[j + p, pl.ds((max(0, delta) * 2 + 1) * B, count), :]
        found = jnp.dot(left, right, preferred_element_type=F32)
        found = found * mask_tile(t_ref, 2 * (k + p), 2 * (j + p), 2)
        given = gk[j + p, pl.ds((2 * delta + 6) * B, 256), :].astype(F32)
        gb[pl.ds(pl.multiple_of(k * 256, 256), 256), pl.ds(pl.multiple_of(j * 256, 256), 256)] = (
            3.0 * given - 2.0 * found
        ).astype(BF16)

    tile_loop(core_ref, tile)

    def finish(j):
        low, count = span(2 * j)
        cols = pl.ds(low * B, count * B)
        right = pk_ref[j + p, :, pl.ds((low + 5 - 2 * j) * B, count * B)]
        total = lax.dot_general(gb[pl.ds(5 * B, 256), cols], right, NT, preferred_element_type=F32)
        total += jnp.dot(
            lhs[:, cols], gb[pl.ds(low * B, count * B), pl.ds(j * 256, 256)],
            preferred_element_type=F32,
        )
        total -= 2.0 * third_s[:, pl.ds(j * 256, 256)]
        for r in range(2):
            for e in range(2):
                slot = 2 * j + e - r
                if 0 <= slot < SLOTS:
                    keep = s_ref[r, slot].astype(F32)
                    grad_ref[r, slot] = total[r * B : r * B + B, e * B : e * B + B] * keep

    for j in range(6):
        in_block(core_ref, functools.partial(finish, j))


SMEM = pl.BlockSpec(memory_space=pltpu.SMEM)
VMEM = pl.BlockSpec(memory_space=pltpu.VMEM)
ANY = pl.BlockSpec(memory_space=pl.ANY)


def flat(blocks, extra=0):
    return jax.ShapeDtypeStruct((blocks * B + extra, B), BF16)


def on_device(density, cotangent, s_mask, t_mask):
    devices = lax.axis_size(AXES)
    core = (lax.axis_index(AXES) % 2).astype(jnp.int32).reshape(1)
    swap = [(i, i ^ 1) for i in range(devices)]

    def send(message, pair):
        return lax.ppermute(message, AXES, route(pair, devices))

    def to_mate(message):
        return lax.ppermute(message, AXES, swap)

    def both_to_mate(messages):
        got = to_mate(jnp.concatenate(messages, axis=0))
        places = [0]
        for message in messages:
            places.append(places[-1] + message.shape[0])
        return [got[a:b] for a, b in zip(places, places[1:])]

    params = pltpu.CompilerParams(vmem_limit_bytes=30 * 1024 * 1024)
    p_pairs = (NEAR2, FAR2, NEAR4)
    packed = pl.pallas_call(
        pack,
        in_specs=[SMEM, SMEM, SMEM, ANY, ANY],
        out_specs=[VMEM] * 10,
        out_shape=[flat(22, MASK_ROWS)]
        + [flat(P_BLOCKS[pair], MASK_ROWS) for pair in p_pairs]
        + [flat(22)]
        + [flat(g_blocks(pair)) for pair in G_PAIRS],
        scratch_shapes=[
            pltpu.VMEM(density.shape, BF16), pltpu.VMEM(cotangent.shape, BF16),
            pltpu.SemaphoreType.DMA((2,)),
        ],
        compiler_params=params,
        name="pack",
    )(core, s_mask, t_mask, density, cotangent)
    p_out, g_out = packed[:4], packed[4:]
    p_far = [send(message, pair) for message, pair in zip(p_out[1:], p_pairs)]
    g_far = [send(message, pair) for message, pair in zip(g_out[1:], G_PAIRS)]
    mate_p = to_mate(p_out[0])
    mate_g = to_mate(g_out[0])
    p_mate = both_to_mate(p_far)
    def zipped(far, mate):
        return [one for both in zip(far, mate) for one in both]

    purified, third, pk, t_all = pl.pallas_call(
        square_kernel,
        in_specs=[SMEM] + [VMEM] * 9,
        out_specs=[VMEM] * 4,
        out_shape=[
            jax.ShapeDtypeStruct((2, SLOTS, B, B), F32),
            jax.ShapeDtypeStruct((256, 1536), F32),
            jax.ShapeDtypeStruct((7, 256, 1536), BF16),
            jax.ShapeDtypeStruct((14 * 16, B), F32),
        ],
        scratch_shapes=[pltpu.VMEM((1536, 1536), BF16), pltpu.VMEM((512, 1536), BF16)],
        cost_estimate=pl.CostEstimate(flops=10**6, bytes_accessed=10**4, transcendentals=0),
        compiler_params=params,
        name="square",
    )(core, p_out[0], mate_p, *zipped(p_far, p_mate), g_out[0])

    *g_far, t_all = lax.optimization_barrier((*g_far, t_all))
    g_mate = [to_mate(g_far[0]), to_mate(g_far[1]), *both_to_mate(g_far[2:])]

    gradient = pl.pallas_call(
        gradient_kernel,
        in_specs=[SMEM, SMEM] + [VMEM] * 16,
        out_specs=VMEM,
        out_shape=jax.ShapeDtypeStruct((2, SLOTS, B, B), F32),
        scratch_shapes=[
            pltpu.VMEM((7, 14 * B, 256), BF16), pltpu.VMEM((1536, 1536), BF16),
            pltpu.VMEM((256, 1536), BF16),
        ],
        cost_estimate=pl.CostEstimate(flops=7 * 10**9, bytes_accessed=16 * 10**6, transcendentals=0),
        compiler_params=params,
        name="gradient",
    )(core, s_mask, g_out[0], mate_g, *zipped(g_far, g_mate), p_out[0], pk, third, t_all)
    return (purified, gradient)


def solution(mesh):
    band = P(AXES, None, None, None)
    in_specs = (band, band, P(AXES, None), P(AXES, None))
    return jax.shard_map(
        on_device, mesh=mesh, in_specs=in_specs, out_specs=(band, band), check_vma=False
    )
```

```python
import functools

import jax
import jax.numpy as jnp
from jax import lax
from jax.experimental import pallas as pl
from jax.experimental.pallas import tpu as pltpu
from jax.sharding import PartitionSpec as P

B = 128
HALF = 5
SLOTS = 11
AXES = ("row", "col")
MASK_ROWS = 32
BF16 = jnp.bfloat16
F32 = jnp.float32

G_OFFSET = 22 * B + MASK_ROWS


def place_in(ts, t):
    return sum(SLOTS - u for u in ts if u < t)


ONE_CHIP, TWO_CHIPS, THREE_CHIPS = (1, 2, 3, 4), (5, 6, 7, 8), (9, 10)
ONE_BLOCKS, TWO_BLOCKS, THREE_BLOCKS = (
    place_in(ts, SLOTS) for ts in (ONE_CHIP, TWO_CHIPS, THREE_CHIPS)
)
N2_ROWS = 13 * B + MASK_ROWS
F2_ROWS = 12 * B + MASK_ROWS


def route(hop, near, devices):
    pairs = []
    for source in range(devices):
        up = (source % 2 == 1) == near
        target = source + hop if up else source - hop
        if 0 <= target < devices:
            pairs.append((source, target))
    return pairs


def rows_of(block, base=0):
    start = block * B + base
    if not isinstance(start, int):
        start = pl.multiple_of(start, MASK_ROWS)
    return pl.ds(start, B)


def masked(values_ref, mask_ref, row, slot):
    keep = mask_ref[row, slot].astype(F32)
    return (values_ref[row, slot].astype(F32) * keep).astype(BF16)


def pack_own(
    core_ref, s_any, t_any, density_any, cotangent_any,
    near2_ref, far2_ref, near4_ref, own_ref, w6_ref,
    density_ref, cotangent_ref, s_ref, t_ref, sems,
):
    first = pltpu.make_async_copy(density_any, density_ref, sems.at[0])
    second = pltpu.make_async_copy(cotangent_any, cotangent_ref, sems.at[1])
    s_copy = pltpu.make_async_copy(s_any, s_ref, sems.at[2])
    t_copy = pltpu.make_async_copy(t_any, t_ref, sems.at[3])
    s_copy.start()
    t_copy.start()
    first.start()
    second.start()
    q = core_ref[0]
    o = 1 - q
    s_copy.wait()
    t_copy.wait()

    line = lax.broadcasted_iota(jnp.int32, (MASK_ROWS, B), 0)
    mask = jnp.zeros((MASK_ROWS, B), F32)
    for row in range(2):
        for slot in range(SLOTS):
            mask = jnp.where(line == row * 16 + slot + 2, t_ref[row, slot].astype(F32), mask)
    mask = mask.astype(BF16)
    for out_ref, count in ((own_ref, 22), (near2_ref, 13), (far2_ref, 12), (near4_ref, 6)):
        out_ref[pl.ds(count * B, MASK_ROWS), :] = mask

    first.wait()

    def put(out_ref, at, row, slot):
        out_ref[rows_of(at), :] = masked(density_ref, s_ref, row, slot)

    for s in range(6):
        put(near2_ref, s, q, 5 * o + s)
        put(near2_ref, 6 + s, o, 5 * o + s)
        put(far2_ref, s, o, 5 * q + s)
        put(far2_ref, 6 + s, q, 5 * q + s)
        put(near4_ref, s, q, 5 * o + s)
    put(near2_ref, 12, q, 10 * q)
    for row in range(2):
        for slot in range(SLOTS):
            put(own_ref, row * SLOTS + slot, row, slot)

    second.wait()
    for row in range(2):
        for slot in range(SLOTS):
            own_ref[rows_of(row * SLOTS + slot, G_OFFSET), :] = masked(
                cotangent_ref, t_ref, row, slot
            )
    at = 0
    for t in THREE_CHIPS:
        row = q if t % 2 else o
        for s in range(SLOTS - t):
            w6_ref[rows_of(at), :] = masked(cotangent_ref, t_ref, row, t * q + s)
            at += 1


def pack_chip(core_ref, own_ref, mate_ref, w2_ref, w4_ref):
    q = core_ref[0]
    o = 1 - q
    for ts, out_ref in ((ONE_CHIP, w2_ref), (TWO_CHIPS, w4_ref)):
        at = 0
        for place, t in enumerate(ts):
            source = own_ref if place < 2 else mate_ref
            row = q if t % 2 else o
            for s in range(SLOTS - t):
                out_ref[rows_of(at), :] = source[
                    rows_of(row * SLOTS + t * q + s, G_OFFSET), :
                ]
                at += 1


def by_side(core, near, received, other):
    return (other, received) if (core == 0) == near else (received, other)


def in_block(core_ref, work):
    pl.when(core_ref[0] >= 0)(work)


def tile_loop(core_ref, body):
    for delta in range(-3, 4):

        def diagonal(delta=delta):
            for j in range(max(0, -delta), min(6, 6 - delta)):
                body(delta, j)

        in_block(core_ref, diagonal)


def mask_tile(t_ref, first_k, first_j, height):
    rows = []
    for k in range(height):
        pieces = []
        for j in range(2):
            line = (first_k + k) * 16 + (first_j + j) - (first_k + k) + HALF + 2
            pieces.append(jnp.broadcast_to(t_ref[pl.ds(line, 1), :], (B, B)))
        rows.append(jnp.concatenate(pieces, axis=1))
    return jnp.concatenate(rows, axis=0)


def span(j0):
    low = max(0, j0 - 5)
    high = min(11, j0 + 6)
    return low, high - low + 1


NT = (((1,), (1,)), ((), ()))


def square_kernel(
    core_ref, own, mate, n2_r, f2_r, n4_r, parts_x,
    purified_ref, third_ref, pk_ref, t_ref,
    sw, lhs,
):
    p = core_ref[0]
    zero = jnp.zeros((B, B), BF16)

    def assemble(core):
        full = (own, mate) if core == 0 else (mate, own)
        n2 = by_side(core, True, (n2_r, 0), (parts_x, 0))
        f2 = by_side(core, False, (f2_r, 0), (parts_x, N2_ROWS))
        n4 = by_side(core, True, (n4_r, 0), (parts_x, N2_ROWS + F2_ROWS))

        def held(k, slot):
            if 5 <= k <= 8:
                return full[(k - 5) // 2][rows_of(((k - 5) % 2) * SLOTS + slot), :]
            side = 0 if k < 5 else 1
            t = 5 - k if k < 5 else k - 8
            at = slot if k < 5 else slot - 5
            ref, base = n2[side] if t <= 2 else f2[side] if t <= 4 else n4[side]
            return ref[rows_of(at if t % 2 else at + 6, base), :]

        def block(k, slot):
            if 5 <= k <= 8 or (k < 5 and slot <= 5) or (k > 8 and slot >= 5):
                return held(k, slot)
            if (k, slot) == (4, 10):
                return n2[0][0][rows_of(12, n2[0][1]), :]
            if (k, slot) == (9, 0):
                return n2[1][0][rows_of(12, n2[1][1]), :]
            return held(k + slot - 5, 10 - slot).T

        for pair in range(core, core + 6):
            for e in range(2):
                rows = pl.ds(e * B, B)
                pk_ref[pair, rows, pl.ds((11 if e == 0 else 0) * B, B)] = zero
                for slot in range(SLOTS):
                    pk_ref[pair, rows, pl.ds((slot + e) * B, B)] = block(2 * pair + e, slot)

        for k in range(14):
            if 5 <= k <= 8:
                part = full[(k - 5) // 2][pl.ds(22 * B, MASK_ROWS), :]
                r = (k - 5) % 2
            else:
                side = 0 if k < 5 else 1
                t = 5 - k if k < 5 else k - 8
                r = (t % 2) if side == 0 else (1 - t % 2)
                (ref, base), count = (
                    (n2[side], 13) if t <= 2 else (f2[side], 12) if t <= 4 else (n4[side], 6)
                )
                part = ref[pl.ds(base + count * B, MASK_ROWS), :]
            t_ref[pl.ds(k * 16, 16), :] = part.astype(F32)[r * 16 : r * 16 + 16, :]

    for core in range(2):
        pl.when(p == core)(functools.partial(assemble, core))

    for r in range(2):
        hole = pl.ds((11 if r == 0 else 0) * B, B)
        lhs[pl.ds(r * B, B), hole] = zero
        lhs[pl.ds((2 + r) * B, B), hole] = zero
        for slot in range(SLOTS):
            cols = pl.ds((slot + r) * B, B)
            lhs[pl.ds(r * B, B), cols] = own[rows_of(r * SLOTS + slot), :]
            lhs[pl.ds((2 + r) * B, B), cols] = own[rows_of(r * SLOTS + slot, G_OFFSET), :]

    def tile(delta, j):
        k = j + delta
        count = (12 - 2 * abs(delta)) * B
        left = pk_ref[k + p, :, pl.ds(max(0, -delta) * 2 * B, count)]
        right = pk_ref[j + p, :, pl.ds(max(0, delta) * 2 * B, count)]
        found = lax.dot_general(left, right, NT, preferred_element_type=F32)
        found = found * mask_tile(t_ref, 2 * (k + p), 2 * (j + p), 2)
        sw[pl.ds(pl.multiple_of(k * 256, 256), 256), pl.ds(pl.multiple_of(j * 256, 256), 256)] = (
            found.astype(BF16)
        )

    tile_loop(core_ref, tile)

    def finish(j):
        low, count = span(2 * j)
        cols = pl.ds(low * B, count * B)
        right = pk_ref[j + p, :, pl.ds((low + 5 - 2 * j) * B, count * B)]
        square = lax.dot_general(lhs[pl.ds(0, 256), cols], right, NT, preferred_element_type=F32)
        both = jnp.dot(
            lhs[:, cols], sw[pl.ds(low * B, count * B), pl.ds(j * 256, 256)],
            preferred_element_type=F32,
        )
        third_ref[:, pl.ds(j * 256, 256)] = both[256:]
        pure = (3.0 * square - 2.0 * both[:256]) * mask_tile(t_ref, 5 + 2 * p, 2 * j + 2 * p, 2)
        for r in range(2):
            for e in range(2):
                slot = 2 * j + e - r
                if 0 <= slot < SLOTS:
                    purified_ref[r, slot] = pure[r * B : r * B + B, e * B : e * B + B]

    for j in range(6):
        in_block(core_ref, functools.partial(finish, j))


def gradient_kernel(
    core_ref, s_ref, own, mate, w2_r, w2_x, w4_r, w6_r, parts_x, pk_ref, third_s, t_ref,
    grad_ref,
    gk, gb, lhs,
):
    p = core_ref[0]
    zero = jnp.zeros((B, B), BF16)

    def assemble(core):
        full = (own, mate) if core == 0 else (mate, own)
        stores = (
            (ONE_CHIP, by_side(core, True, (w2_r, 0), (w2_x, 0))),
            (TWO_CHIPS, by_side(core, True, (w4_r, 0), (parts_x, 0))),
            (THREE_CHIPS, by_side(core, True, (w6_r, 0), (parts_x, TWO_BLOCKS * B))),
        )

        def block(m, slot):
            if 10 <= m <= 13:
                return full[(m - 10) // 2][rows_of(((m - 10) % 2) * SLOTS + slot, G_OFFSET), :]
            side = 0 if m < 10 else 1
            t = 10 - m if m < 10 else m - 13
            at = slot - t if side == 0 else slot
            ts, sides = stores[(t - 1) // 4]
            ref, base = sides[side]
            return ref[rows_of(at + place_in(ts, t), base), :]

        for pair in range(core, core + 6):
            for e in range(2):
                cols = pl.ds(e * B, B)
                for hole in ((0, 12, 13), (0, 1, 13))[e]:
                    gk[pair, pl.ds(hole * B, B), cols] = zero
                j = 2 * pair + e
                for m in range(j, j + 11):
                    gk[pair, pl.ds((m - 2 * pair + 1) * B, B), cols] = block(m, j - m + 10)

    for core in range(2):
        pl.when(p == core)(functools.partial(assemble, core))

    for r in range(2):
        lhs[pl.ds(r * B, B), pl.ds((11 if r == 0 else 0) * B, B)] = zero
        for slot in range(SLOTS):
            lhs[pl.ds(r * B, B), pl.ds((slot + r) * B, B)] = own[rows_of(r * SLOTS + slot), :]

    def tile(delta, j):
        k = j + delta
        count = (12 - 2 * abs(delta)) * B
        left = pk_ref[k + p, :, pl.ds(max(0, -delta) * 2 * B, count)]
        right = gk[j + p, pl.ds((max(0, delta) * 2 + 1) * B, count), :]
        found = jnp.dot(left, right, preferred_element_type=F32)
        found = found * mask_tile(t_ref, 2 * (k + p), 2 * (j + p), 2)
        given = gk[j + p, pl.ds((2 * delta + 6) * B, 256), :].astype(F32)
        gb[pl.ds(pl.multiple_of(k * 256, 256), 256), pl.ds(pl.multiple_of(j * 256, 256), 256)] = (
            3.0 * given - 2.0 * found
        ).astype(BF16)

    tile_loop(core_ref, tile)

    def finish(j):
        low, count = span(2 * j)
        cols = pl.ds(low * B, count * B)
        right = pk_ref[j + p, :, pl.ds((low + 5 - 2 * j) * B, count * B)]
        total = lax.dot_general(gb[pl.ds(5 * B, 256), cols], right, NT, preferred_element_type=F32)
        total += jnp.dot(
            lhs[:, cols], gb[pl.ds(low * B, count * B), pl.ds(j * 256, 256)],
            preferred_element_type=F32,
        )
        total -= 2.0 * third_s[:, pl.ds(j * 256, 256)]
        for r in range(2):
            for e in range(2):
                slot = 2 * j + e - r
                if 0 <= slot < SLOTS:
                    keep = s_ref[r, slot].astype(F32)
                    grad_ref[r, slot] = total[r * B : r * B + B, e * B : e * B + B] * keep

    for j in range(6):
        in_block(core_ref, functools.partial(finish, j))


SMEM = pl.BlockSpec(memory_space=pltpu.SMEM)
VMEM = pl.BlockSpec(memory_space=pltpu.VMEM)
HBM = pl.BlockSpec(memory_space=pltpu.HBM)


def flat(blocks, extra=0):
    return jax.ShapeDtypeStruct((blocks * B + extra, B), BF16)


def on_device(density, cotangent, s_mask, t_mask):
    devices = lax.axis_size(AXES)
    core = (lax.axis_index(AXES) % 2).astype(jnp.int32).reshape(1)
    swap = [(i, i ^ 1) for i in range(devices)]

    def send(message, hop, near=True):
        return lax.ppermute(message, AXES, route(hop, near, devices))

    def to_mate(*messages):
        return lax.ppermute(jnp.concatenate(messages, axis=0), AXES, swap)

    params = pltpu.CompilerParams(vmem_limit_bytes=30 * 1024 * 1024)
    n2, f2, n4, own, w6 = pl.pallas_call(
        pack_own,
        in_specs=[SMEM, HBM, HBM, HBM, HBM],
        out_specs=[VMEM] * 5,
        out_shape=[
            flat(13, MASK_ROWS), flat(12, MASK_ROWS), flat(6, MASK_ROWS), flat(44, MASK_ROWS),
            flat(THREE_BLOCKS),
        ],
        scratch_shapes=[
            pltpu.VMEM(density.shape, BF16), pltpu.VMEM(cotangent.shape, BF16),
            pltpu.SMEM((2, SLOTS), jnp.int32), pltpu.SMEM((2, SLOTS), jnp.int32),
            pltpu.SemaphoreType.DMA((4,)),
        ],
        compiler_params=pltpu.CompilerParams(vmem_limit_bytes=62 * 1024 * 1024),
        name="pack_own",
    )(core, s_mask, t_mask, density, cotangent)
    n2_r = send(n2, 2)
    f2_r = send(f2, 2, near=False)
    n4_r = send(n4, 4)
    mate = to_mate(own)
    w2, w4 = pl.pallas_call(
        pack_chip,
        in_specs=[SMEM, VMEM, VMEM],
        out_specs=[VMEM] * 2,
        out_shape=[flat(ONE_BLOCKS), flat(TWO_BLOCKS)],
        compiler_params=params,
        name="pack_chip",
    )(core, own, mate)
    f2_r, w2 = lax.optimization_barrier((f2_r, w2))
    w2_r = send(w2, 2)
    w4_r = send(w4, 4)
    w6_r = send(w6, 6)
    p_parts = to_mate(n2_r, f2_r, n4_r)

    purified, third, pk, t_all = pl.pallas_call(
        square_kernel,
        in_specs=[SMEM] + [VMEM] * 6,
        out_specs=[VMEM] * 4,
        out_shape=[
            jax.ShapeDtypeStruct((2, SLOTS, B, B), F32),
            jax.ShapeDtypeStruct((256, 1536), F32),
            jax.ShapeDtypeStruct((7, 256, 1536), BF16),
            jax.ShapeDtypeStruct((14 * 16, B), F32),
        ],
        scratch_shapes=[pltpu.VMEM((1536, 1536), BF16), pltpu.VMEM((512, 1536), BF16)],
        cost_estimate=pl.CostEstimate(flops=10**6, bytes_accessed=10**4, transcendentals=0),
        compiler_params=params,
        name="square",
    )(core, own, mate, n2_r, f2_r, n4_r, p_parts)

    w2_r, w4_g, w6_r, t_all = lax.optimization_barrier((w2_r, w4_r, w6_r, t_all))
    g_parts = to_mate(w4_g, w6_r)
    w2_x = to_mate(w2_r)

    gradient = pl.pallas_call(
        gradient_kernel,
        in_specs=[SMEM, SMEM] + [VMEM] * 10,
        out_specs=VMEM,
        out_shape=jax.ShapeDtypeStruct((2, SLOTS, B, B), F32),
        scratch_shapes=[
            pltpu.VMEM((7, 14 * B, 256), BF16), pltpu.VMEM((1536, 1536), BF16),
            pltpu.VMEM((256, 1536), BF16),
        ],
        cost_estimate=pl.CostEstimate(flops=7 * 10**9, bytes_accessed=16 * 10**6, transcendentals=0),
        compiler_params=params,
        name="gradient",
    )(core, s_mask, own, mate, w2_r, w2_x, w4_g, w6_r, g_parts, pk, third, t_all)
    return (purified, gradient)


def solution(mesh):
    band = P(AXES, None, None, None)
    in_specs = (band, band, P(AXES, None), P(AXES, None))
    return jax.shard_map(
        on_device, mesh=mesh, in_specs=in_specs, out_specs=(band, band), check_vma=False
    )
```

```python
import functools

import jax
import jax.numpy as jnp
from jax import lax
from jax.experimental import pallas as pl
from jax.experimental.pallas import tpu as pltpu
from jax.sharding import PartitionSpec as P

B = 128
HALF = 5
SLOTS = 11
AXES = ("row", "col")
MASK_ROWS = 32
BF16 = jnp.bfloat16
F32 = jnp.float32

G_OFFSET = 22 * B + MASK_ROWS


def place_in(ts, t):
    return sum(SLOTS - u for u in ts if u < t)


ONE_CHIP, TWO_CHIPS, THREE_CHIPS = (1, 2, 3, 4), (5, 6, 7, 8), (9, 10)
ONE_BLOCKS, TWO_BLOCKS, THREE_BLOCKS = (
    place_in(ts, SLOTS) for ts in (ONE_CHIP, TWO_CHIPS, THREE_CHIPS)
)
N2_ROWS = 13 * B + MASK_ROWS
F2_ROWS = 12 * B + MASK_ROWS


def route(hop, near, devices):
    pairs = []
    for source in range(devices):
        up = (source % 2 == 1) == near
        target = source + hop if up else source - hop
        if 0 <= target < devices:
            pairs.append((source, target))
    return pairs


def rows_of(block, base=0):
    start = block * B + base
    if not isinstance(start, int):
        start = pl.multiple_of(start, MASK_ROWS)
    return pl.ds(start, B)


def masked(values_ref, mask_ref, row, slot):
    keep = mask_ref[row, slot].astype(F32)
    return (values_ref[row, slot].astype(F32) * keep).astype(BF16)


def pack_own(
    core_ref, s_any, t_any, density_any, cotangent_any,
    near2_ref, far2_ref, near4_ref, own_ref, w6_ref,
    density_ref, cotangent_ref, s_ref, t_ref, sems,
):
    first = pltpu.make_async_copy(density_any, density_ref, sems.at[0])
    second = pltpu.make_async_copy(cotangent_any, cotangent_ref, sems.at[1])
    s_copy = pltpu.make_async_copy(s_any, s_ref, sems.at[2])
    t_copy = pltpu.make_async_copy(t_any, t_ref, sems.at[3])
    s_copy.start()
    t_copy.start()
    first.start()
    second.start()
    q = core_ref[0]
    o = 1 - q
    s_copy.wait()
    t_copy.wait()

    line = lax.broadcasted_iota(jnp.int32, (MASK_ROWS, B), 0)
    mask = jnp.zeros((MASK_ROWS, B), F32)
    for row in range(2):
        for slot in range(SLOTS):
            mask = jnp.where(line == row * 16 + slot + 2, t_ref[row, slot].astype(F32), mask)
    mask = mask.astype(BF16)
    for out_ref, count in ((own_ref, 22), (near2_ref, 13), (far2_ref, 12), (near4_ref, 6)):
        out_ref[pl.ds(count * B, MASK_ROWS), :] = mask

    first.wait()

    def put(out_ref, at, row, slot):
        out_ref[rows_of(at), :] = masked(density_ref, s_ref, row, slot)

    for s in range(6):
        put(near2_ref, s, q, 5 * o + s)
        put(near2_ref, 6 + s, o, 5 * o + s)
        put(far2_ref, s, o, 5 * q + s)
        put(far2_ref, 6 + s, q, 5 * q + s)
        put(near4_ref, s, q, 5 * o + s)
    put(near2_ref, 12, q, 10 * q)
    for row in range(2):
        for slot in range(SLOTS):
            put(own_ref, row * SLOTS + slot, row, slot)

    second.wait()
    for row in range(2):
        for slot in range(SLOTS):
            own_ref[rows_of(row * SLOTS + slot, G_OFFSET), :] = masked(
                cotangent_ref, t_ref, row, slot
            )
    at = 0
    for t in THREE_CHIPS:
        row = q if t % 2 else o
        for s in range(SLOTS - t):
            w6_ref[rows_of(at), :] = masked(cotangent_ref, t_ref, row, t * q + s)
            at += 1


def pack_chip(core_ref, own_ref, mate_ref, w2_ref, w4_ref):
    q = core_ref[0]
    o = 1 - q
    for ts, out_ref in ((ONE_CHIP, w2_ref), (TWO_CHIPS, w4_ref)):
        at = 0
        for place, t in enumerate(ts):
            source = own_ref if place < 2 else mate_ref
            row = q if t % 2 else o
            for s in range(SLOTS - t):
                out_ref[rows_of(at), :] = source[
                    rows_of(row * SLOTS + t * q + s, G_OFFSET), :
                ]
                at += 1


def by_side(core, near, received, other):
    return (other, received) if (core == 0) == near else (received, other)


def in_block(core_ref, work):
    pl.when(core_ref[0] >= 0)(work)


def tile_loop(core_ref, body):
    for delta in range(-3, 4):

        def diagonal(delta=delta):
            for j in range(max(0, -delta), min(6, 6 - delta)):
                body(delta, j)

        in_block(core_ref, diagonal)


def mask_tile(t_ref, first_k, first_j, height):
    rows = []
    for k in range(height):
        pieces = []
        for j in range(2):
            line = (first_k + k) * 16 + (first_j + j) - (first_k + k) + HALF + 2
            pieces.append(jnp.broadcast_to(t_ref[pl.ds(line, 1), :], (B, B)))
        rows.append(jnp.concatenate(pieces, axis=1))
    return jnp.concatenate(rows, axis=0)


def span(j0):
    low = max(0, j0 - 5)
    high = min(11, j0 + 6)
    return low, high - low + 1


NT = (((1,), (1,)), ((), ()))


def square_kernel(
    core_ref, own, mate, n2_r, f2_r, n4_r, parts_x,
    purified_ref, third_ref, pk_ref, t_ref,
    sw, lhs,
):
    p = core_ref[0]
    zero = jnp.zeros((B, B), BF16)

    def assemble(core):
        full = (own, mate) if core == 0 else (mate, own)
        n2 = by_side(core, True, (n2_r, 0), (parts_x, 0))
        f2 = by_side(core, False, (f2_r, 0), (parts_x, N2_ROWS))
        n4 = by_side(core, True, (n4_r, 0), (parts_x, N2_ROWS + F2_ROWS))

        def held(k, slot):
            if 5 <= k <= 8:
                return full[(k - 5) // 2][rows_of(((k - 5) % 2) * SLOTS + slot), :]
            side = 0 if k < 5 else 1
            t = 5 - k if k < 5 else k - 8
            at = slot if k < 5 else slot - 5
            ref, base = n2[side] if t <= 2 else f2[side] if t <= 4 else n4[side]
            return ref[rows_of(at if t % 2 else at + 6, base), :]

        def block(k, slot):
            if 5 <= k <= 8 or (k < 5 and slot <= 5) or (k > 8 and slot >= 5):
                return held(k, slot)
            if (k, slot) == (4, 10):
                return n2[0][0][rows_of(12, n2[0][1]), :]
            if (k, slot) == (9, 0):
                return n2[1][0][rows_of(12, n2[1][1]), :]
            return held(k + slot - 5, 10 - slot).T

        for pair in range(core, core + 6):
            for e in range(2):
                rows = pl.ds(e * B, B)
                pk_ref[pair, rows, pl.ds((11 if e == 0 else 0) * B, B)] = zero
                for slot in range(SLOTS):
                    pk_ref[pair, rows, pl.ds((slot + e) * B, B)] = block(2 * pair + e, slot)

        for k in range(14):
            if 5 <= k <= 8:
                part = full[(k - 5) // 2][pl.ds(22 * B, MASK_ROWS), :]
                r = (k - 5) % 2
            else:
                side = 0 if k < 5 else 1
                t = 5 - k if k < 5 else k - 8
                r = (t % 2) if side == 0 else (1 - t % 2)
                (ref, base), count = (
                    (n2[side], 13) if t <= 2 else (f2[side], 12) if t <= 4 else (n4[side], 6)
                )
                part = ref[pl.ds(base + count * B, MASK_ROWS), :]
            t_ref[pl.ds(k * 16, 16), :] = part.astype(F32)[r * 16 : r * 16 + 16, :]

    for core in range(2):
        pl.when(p == core)(functools.partial(assemble, core))

    for r in range(2):
        hole = pl.ds((11 if r == 0 else 0) * B, B)
        lhs[pl.ds(r * B, B), hole] = zero
        lhs[pl.ds((2 + r) * B, B), hole] = zero
        for slot in range(SLOTS):
            cols = pl.ds((slot + r) * B, B)
            lhs[pl.ds(r * B, B), cols] = own[rows_of(r * SLOTS + slot), :]
            lhs[pl.ds((2 + r) * B, B), cols] = own[rows_of(r * SLOTS + slot, G_OFFSET), :]

    def tile(delta, j):
        k = j + delta
        count = (12 - 2 * abs(delta)) * B
        left = pk_ref[k + p, :, pl.ds(max(0, -delta) * 2 * B, count)]
        right = pk_ref[j + p, :, pl.ds(max(0, delta) * 2 * B, count)]
        found = lax.dot_general(left, right, NT, preferred_element_type=F32)
        found = found * mask_tile(t_ref, 2 * (k + p), 2 * (j + p), 2)
        sw[pl.ds(pl.multiple_of(k * 256, 256), 256), pl.ds(pl.multiple_of(j * 256, 256), 256)] = (
            found.astype(BF16)
        )

    tile_loop(core_ref, tile)

    def finish(j):
        low, count = span(2 * j)
        cols = pl.ds(low * B, count * B)
        right = pk_ref[j + p, :, pl.ds((low + 5 - 2 * j) * B, count * B)]
        square = lax.dot_general(lhs[pl.ds(0, 256), cols], right, NT, preferred_element_type=F32)
        both = jnp.dot(
            lhs[:, cols], sw[pl.ds(low * B, count * B), pl.ds(j * 256, 256)],
            preferred_element_type=F32,
        )
        third_ref[:, pl.ds(j * 256, 256)] = both[256:]
        pure = (3.0 * square - 2.0 * both[:256]) * mask_tile(t_ref, 5 + 2 * p, 2 * j + 2 * p, 2)
        for r in range(2):
            for e in range(2):
                slot = 2 * j + e - r
                if 0 <= slot < SLOTS:
                    purified_ref[r, slot] = pure[r * B : r * B + B, e * B : e * B + B]

    for j in range(6):
        in_block(core_ref, functools.partial(finish, j))


def gradient_kernel(
    core_ref, s_ref, own, mate, w2_r, w2_x, w4_r, w6_r, parts_x, pk_ref, third_s, t_ref,
    grad_ref,
    gk, gb, lhs,
):
    p = core_ref[0]
    zero = jnp.zeros((B, B), BF16)

    def assemble(core):
        full = (own, mate) if core == 0 else (mate, own)
        stores = (
            (ONE_CHIP, by_side(core, True, (w2_r, 0), (w2_x, 0))),
            (TWO_CHIPS, by_side(core, True, (w4_r, 0), (parts_x, 0))),
            (THREE_CHIPS, by_side(core, True, (w6_r, 0), (parts_x, TWO_BLOCKS * B))),
        )

        def block(m, slot):
            if 10 <= m <= 13:
                return full[(m - 10) // 2][rows_of(((m - 10) % 2) * SLOTS + slot, G_OFFSET), :]
            side = 0 if m < 10 else 1
            t = 10 - m if m < 10 else m - 13
            at = slot - t if side == 0 else slot
            ts, sides = stores[(t - 1) // 4]
            ref, base = sides[side]
            return ref[rows_of(at + place_in(ts, t), base), :]

        for pair in range(core, core + 6):
            for e in range(2):
                cols = pl.ds(e * B, B)
                for hole in ((0, 12, 13), (0, 1, 13))[e]:
                    gk[pair, pl.ds(hole * B, B), cols] = zero
                j = 2 * pair + e
                for m in range(j, j + 11):
                    gk[pair, pl.ds((m - 2 * pair + 1) * B, B), cols] = block(m, j - m + 10)

    for core in range(2):
        pl.when(p == core)(functools.partial(assemble, core))

    for r in range(2):
        lhs[pl.ds(r * B, B), pl.ds((11 if r == 0 else 0) * B, B)] = zero
        for slot in range(SLOTS):
            lhs[pl.ds(r * B, B), pl.ds((slot + r) * B, B)] = own[rows_of(r * SLOTS + slot), :]

    def tile(delta, j):
        k = j + delta
        count = (12 - 2 * abs(delta)) * B
        left = pk_ref[k + p, :, pl.ds(max(0, -delta) * 2 * B, count)]
        right = gk[j + p, pl.ds((max(0, delta) * 2 + 1) * B, count), :]
        found = jnp.dot(left, right, preferred_element_type=F32)
        found = found * mask_tile(t_ref, 2 * (k + p), 2 * (j + p), 2)
        given = gk[j + p, pl.ds((2 * delta + 6) * B, 256), :].astype(F32)
        gb[pl.ds(pl.multiple_of(k * 256, 256), 256), pl.ds(pl.multiple_of(j * 256, 256), 256)] = (
            3.0 * given - 2.0 * found
        ).astype(BF16)

    tile_loop(core_ref, tile)

    def finish(j):
        low, count = span(2 * j)
        cols = pl.ds(low * B, count * B)
        right = pk_ref[j + p, :, pl.ds((low + 5 - 2 * j) * B, count * B)]
        total = lax.dot_general(gb[pl.ds(5 * B, 256), cols], right, NT, preferred_element_type=F32)
        total += jnp.dot(
            lhs[:, cols], gb[pl.ds(low * B, count * B), pl.ds(j * 256, 256)],
            preferred_element_type=F32,
        )
        total -= 2.0 * third_s[:, pl.ds(j * 256, 256)]
        for r in range(2):
            for e in range(2):
                slot = 2 * j + e - r
                if 0 <= slot < SLOTS:
                    keep = s_ref[r, slot].astype(F32)
                    grad_ref[r, slot] = total[r * B : r * B + B, e * B : e * B + B] * keep

    for j in range(6):
        in_block(core_ref, functools.partial(finish, j))


SMEM = pl.BlockSpec(memory_space=pltpu.SMEM)
VMEM = pl.BlockSpec(memory_space=pltpu.VMEM)
HBM = pl.BlockSpec(memory_space=pltpu.HBM)


def flat(blocks, extra=0):
    return jax.ShapeDtypeStruct((blocks * B + extra, B), BF16)


def on_device(density, cotangent, s_mask, t_mask):
    devices = lax.axis_size(AXES)
    core = (lax.axis_index(AXES) % 2).astype(jnp.int32).reshape(1)
    swap = [(i, i ^ 1) for i in range(devices)]

    def send(message, hop, near=True):
        return lax.ppermute(message, AXES, route(hop, near, devices))

    def to_mate(*messages):
        return lax.ppermute(jnp.concatenate(messages, axis=0), AXES, swap)

    params = pltpu.CompilerParams(vmem_limit_bytes=30 * 1024 * 1024)
    n2, f2, n4, own, w6 = pl.pallas_call(
        pack_own,
        in_specs=[SMEM, HBM, HBM, HBM, HBM],
        out_specs=[VMEM] * 5,
        out_shape=[
            flat(13, MASK_ROWS), flat(12, MASK_ROWS), flat(6, MASK_ROWS), flat(44, MASK_ROWS),
            flat(THREE_BLOCKS),
        ],
        scratch_shapes=[
            pltpu.VMEM(density.shape, BF16), pltpu.VMEM(cotangent.shape, BF16),
            pltpu.SMEM((2, SLOTS), jnp.int32), pltpu.SMEM((2, SLOTS), jnp.int32),
            pltpu.SemaphoreType.DMA((4,)),
        ],
        compiler_params=pltpu.CompilerParams(vmem_limit_bytes=62 * 1024 * 1024),
        name="pack_own",
    )(core, s_mask, t_mask, density, cotangent)
    n2_r = send(n2, 2)
    f2_r = send(f2, 2, near=False)
    n4_r = send(n4, 4)
    mate = to_mate(own)
    w2, w4 = pl.pallas_call(
        pack_chip,
        in_specs=[SMEM, VMEM, VMEM],
        out_specs=[VMEM] * 2,
        out_shape=[flat(ONE_BLOCKS), flat(TWO_BLOCKS)],
        compiler_params=params,
        name="pack_chip",
    )(core, own, mate)
    w6_r = send(w6, 6)
    f2_r, w6_r, w2 = lax.optimization_barrier((f2_r, w6_r, w2))
    w2_r = send(w2, 2)
    w4_r = send(w4, 4)
    p_parts = to_mate(n2_r, f2_r, n4_r)

    purified, third, pk, t_all = pl.pallas_call(
        square_kernel,
        in_specs=[SMEM] + [VMEM] * 6,
        out_specs=[VMEM] * 4,
        out_shape=[
            jax.ShapeDtypeStruct((2, SLOTS, B, B), F32),
            jax.ShapeDtypeStruct((256, 1536), F32),
            jax.ShapeDtypeStruct((7, 256, 1536), BF16),
            jax.ShapeDtypeStruct((14 * 16, B), F32),
        ],
        scratch_shapes=[pltpu.VMEM((1536, 1536), BF16), pltpu.VMEM((512, 1536), BF16)],
        cost_estimate=pl.CostEstimate(flops=10**6, bytes_accessed=10**4, transcendentals=0),
        compiler_params=params,
        name="square",
    )(core, own, mate, n2_r, f2_r, n4_r, p_parts)

    w2_r, w4_g, w6_r, t_all = lax.optimization_barrier((w2_r, w4_r, w6_r, t_all))
    g_parts = to_mate(w4_g, w6_r)
    w2_x = to_mate(w2_r)

    gradient = pl.pallas_call(
        gradient_kernel,
        in_specs=[SMEM, SMEM] + [VMEM] * 10,
        out_specs=VMEM,
        out_shape=jax.ShapeDtypeStruct((2, SLOTS, B, B), F32),
        scratch_shapes=[
            pltpu.VMEM((7, 14 * B, 256), BF16), pltpu.VMEM((1536, 1536), BF16),
            pltpu.VMEM((256, 1536), BF16),
        ],
        cost_estimate=pl.CostEstimate(flops=7 * 10**9, bytes_accessed=16 * 10**6, transcendentals=0),
        compiler_params=params,
        name="gradient",
    )(core, s_mask, own, mate, w2_r, w2_x, w4_g, w6_r, g_parts, pk, third, t_all)
    return (purified, gradient)


def solution(mesh):
    band = P(AXES, None, None, None)
    in_specs = (band, band, P(AXES, None), P(AXES, None))
    return jax.shard_map(
        on_device, mesh=mesh, in_specs=in_specs, out_specs=(band, band), check_vma=False
    )
```

```python
import functools

import jax
import jax.numpy as jnp
from jax import lax
from jax.experimental import pallas as pl
from jax.experimental.pallas import tpu as pltpu
from jax.sharding import PartitionSpec as P

B = 128
HALF = 5
SLOTS = 11
AXES = ("row", "col")
MASK_ROWS = 32
BF16 = jnp.bfloat16
F32 = jnp.float32

G_OFFSET = 22 * B + MASK_ROWS


def place_in(ts, t):
    return sum(SLOTS - u for u in ts if u < t)


ONE_CHIP, TWO_CHIPS, THREE_CHIPS = (1, 2, 3, 4), (5, 6, 7, 8), (9, 10)
ONE_BLOCKS, TWO_BLOCKS, THREE_BLOCKS = (
    place_in(ts, SLOTS) for ts in (ONE_CHIP, TWO_CHIPS, THREE_CHIPS)
)
N2_ROWS = 13 * B + MASK_ROWS
F2_ROWS = 12 * B + MASK_ROWS


def route(hop, near, devices):
    pairs = []
    for source in range(devices):
        up = (source % 2 == 1) == near
        target = source + hop if up else source - hop
        if 0 <= target < devices:
            pairs.append((source, target))
    return pairs


def rows_of(block, base=0):
    start = block * B + base
    if not isinstance(start, int):
        start = pl.multiple_of(start, MASK_ROWS)
    return pl.ds(start, B)


def masked(values_ref, mask_ref, row, slot):
    keep = mask_ref[row, slot].astype(F32)
    return (values_ref[row, slot].astype(F32) * keep).astype(BF16)


def pack_own(
    core_ref, s_any, t_any, density_any, cotangent_any,
    near2_ref, far2_ref, near4_ref, own_ref, w6_ref,
    density_ref, cotangent_ref, s_ref, t_ref, sems,
):
    first = pltpu.make_async_copy(density_any, density_ref, sems.at[0])
    second = pltpu.make_async_copy(cotangent_any, cotangent_ref, sems.at[1])
    s_copy = pltpu.make_async_copy(s_any, s_ref, sems.at[2])
    t_copy = pltpu.make_async_copy(t_any, t_ref, sems.at[3])
    s_copy.start()
    t_copy.start()
    first.start()
    second.start()
    q = core_ref[0]
    o = 1 - q
    s_copy.wait()
    t_copy.wait()

    line = lax.broadcasted_iota(jnp.int32, (MASK_ROWS, B), 0)
    mask = jnp.zeros((MASK_ROWS, B), F32)
    for row in range(2):
        for slot in range(SLOTS):
            mask = jnp.where(line == row * 16 + slot + 2, t_ref[row, slot].astype(F32), mask)
    mask = mask.astype(BF16)
    for out_ref, count in ((own_ref, 22), (near2_ref, 13), (far2_ref, 12), (near4_ref, 6)):
        out_ref[pl.ds(count * B, MASK_ROWS), :] = mask

    first.wait()

    def put(out_ref, at, row, slot):
        out_ref[rows_of(at), :] = masked(density_ref, s_ref, row, slot)

    for s in range(6):
        put(near2_ref, s, q, 5 * o + s)
        put(near2_ref, 6 + s, o, 5 * o + s)
        put(far2_ref, s, o, 5 * q + s)
        put(far2_ref, 6 + s, q, 5 * q + s)
        put(near4_ref, s, q, 5 * o + s)
    put(near2_ref, 12, q, 10 * q)
    for row in range(2):
        for slot in range(SLOTS):
            put(own_ref, row * SLOTS + slot, row, slot)

    second.wait()
    for row in range(2):
        for slot in range(SLOTS):
            own_ref[rows_of(row * SLOTS + slot, G_OFFSET), :] = masked(
                cotangent_ref, t_ref, row, slot
            )
    at = 0
    for t in THREE_CHIPS:
        row = q if t % 2 else o
        for s in range(SLOTS - t):
            w6_ref[rows_of(at), :] = masked(cotangent_ref, t_ref, row, t * q + s)
            at += 1


def pack_chip(core_ref, own_ref, mate_ref, w2_ref, w4_ref):
    q = core_ref[0]
    o = 1 - q
    for ts, out_ref in ((ONE_CHIP, w2_ref), (TWO_CHIPS, w4_ref)):
        at = 0
        for place, t in enumerate(ts):
            source = own_ref if place < 2 else mate_ref
            row = q if t % 2 else o
            for s in range(SLOTS - t):
                out_ref[rows_of(at), :] = source[
                    rows_of(row * SLOTS + t * q + s, G_OFFSET), :
                ]
                at += 1


def by_side(core, near, received, other):
    return (other, received) if (core == 0) == near else (received, other)


def in_block(core_ref, work):
    pl.when(core_ref[0] >= 0)(work)


def tile_loop(core_ref, body):
    for delta in range(-3, 4):

        def diagonal(delta=delta):
            for j in range(max(0, -delta), min(6, 6 - delta)):
                body(delta, j)

        in_block(core_ref, diagonal)


def mask_tile(t_ref, first_k, first_j, height):
    rows = []
    for k in range(height):
        pieces = []
        for j in range(2):
            line = (first_k + k) * 16 + (first_j + j) - (first_k + k) + HALF + 2
            pieces.append(jnp.broadcast_to(t_ref[pl.ds(line, 1), :], (B, B)))
        rows.append(jnp.concatenate(pieces, axis=1))
    return jnp.concatenate(rows, axis=0)


def span(j0):
    low = max(0, j0 - 5)
    high = min(11, j0 + 6)
    return low, high - low + 1


NT = (((1,), (1,)), ((), ()))


def square_kernel(
    core_ref, own, mate, n2_r, f2_r, n4_r, parts_x,
    purified_ref, third_ref, pk_ref, t_ref,
    sw, lhs,
):
    p = core_ref[0]
    zero = jnp.zeros((B, B), BF16)

    def assemble(core):
        full = (own, mate) if core == 0 else (mate, own)
        n2 = by_side(core, True, (n2_r, 0), (parts_x, 0))
        f2 = by_side(core, False, (f2_r, 0), (parts_x, N2_ROWS))
        n4 = by_side(core, True, (n4_r, 0), (parts_x, N2_ROWS + F2_ROWS))

        def held(k, slot):
            if 5 <= k <= 8:
                return full[(k - 5) // 2][rows_of(((k - 5) % 2) * SLOTS + slot), :]
            side = 0 if k < 5 else 1
            t = 5 - k if k < 5 else k - 8
            at = slot if k < 5 else slot - 5
            ref, base = n2[side] if t <= 2 else f2[side] if t <= 4 else n4[side]
            return ref[rows_of(at if t % 2 else at + 6, base), :]

        def block(k, slot):
            if 5 <= k <= 8 or (k < 5 and slot <= 5) or (k > 8 and slot >= 5):
                return held(k, slot)
            if (k, slot) == (4, 10):
                return n2[0][0][rows_of(12, n2[0][1]), :]
            if (k, slot) == (9, 0):
                return n2[1][0][rows_of(12, n2[1][1]), :]
            return held(k + slot - 5, 10 - slot).T

        for pair in range(core, core + 6):
            for e in range(2):
                rows = pl.ds(e * B, B)
                pk_ref[pair, rows, pl.ds((11 if e == 0 else 0) * B, B)] = zero
                for slot in range(SLOTS):
                    pk_ref[pair, rows, pl.ds((slot + e) * B, B)] = block(2 * pair + e, slot)

        for k in range(14):
            if 5 <= k <= 8:
                part = full[(k - 5) // 2][pl.ds(22 * B, MASK_ROWS), :]
                r = (k - 5) % 2
            else:
                side = 0 if k < 5 else 1
                t = 5 - k if k < 5 else k - 8
                r = (t % 2) if side == 0 else (1 - t % 2)
                (ref, base), count = (
                    (n2[side], 13) if t <= 2 else (f2[side], 12) if t <= 4 else (n4[side], 6)
                )
                part = ref[pl.ds(base + count * B, MASK_ROWS), :]
            t_ref[pl.ds(k * 16, 16), :] = part.astype(F32)[r * 16 : r * 16 + 16, :]

    for core in range(2):
        pl.when(p == core)(functools.partial(assemble, core))

    for r in range(2):
        hole = pl.ds((11 if r == 0 else 0) * B, B)
        lhs[pl.ds(r * B, B), hole] = zero
        lhs[pl.ds((2 + r) * B, B), hole] = zero
        for slot in range(SLOTS):
            cols = pl.ds((slot + r) * B, B)
            lhs[pl.ds(r * B, B), cols] = own[rows_of(r * SLOTS + slot), :]
            lhs[pl.ds((2 + r) * B, B), cols] = own[rows_of(r * SLOTS + slot, G_OFFSET), :]

    def tile(delta, j):
        k = j + delta
        count = (12 - 2 * abs(delta)) * B
        left = pk_ref[k + p, :, pl.ds(max(0, -delta) * 2 * B, count)]
        right = pk_ref[j + p, :, pl.ds(max(0, delta) * 2 * B, count)]
        found = lax.dot_general(left, right, NT, preferred_element_type=F32)
        found = found * mask_tile(t_ref, 2 * (k + p), 2 * (j + p), 2)
        sw[pl.ds(pl.multiple_of(k * 256, 256), 256), pl.ds(pl.multiple_of(j * 256, 256), 256)] = (
            found.astype(BF16)
        )

    tile_loop(core_ref, tile)

    def finish(j):
        low, count = span(2 * j)
        cols = pl.ds(low * B, count * B)
        right = pk_ref[j + p, :, pl.ds((low + 5 - 2 * j) * B, count * B)]
        square = lax.dot_general(lhs[pl.ds(0, 256), cols], right, NT, preferred_element_type=F32)
        both = jnp.dot(
            lhs[:, cols], sw[pl.ds(low * B, count * B), pl.ds(j * 256, 256)],
            preferred_element_type=F32,
        )
        third_ref[:, pl.ds(j * 256, 256)] = both[256:]
        pure = (3.0 * square - 2.0 * both[:256]) * mask_tile(t_ref, 5 + 2 * p, 2 * j + 2 * p, 2)
        for r in range(2):
            for e in range(2):
                slot = 2 * j + e - r
                if 0 <= slot < SLOTS:
                    purified_ref[r, slot] = pure[r * B : r * B + B, e * B : e * B + B]

    for j in range(6):
        in_block(core_ref, functools.partial(finish, j))


def gradient_kernel(
    core_ref, s_ref, own, mate, w2_r, w2_x, w4_r, w6_r, parts_x, pk_ref, third_s, t_ref,
    grad_any,
    gk, gb, lhs, grad_ref, sems,
):
    p = core_ref[0]
    zero = jnp.zeros((B, B), BF16)

    def assemble(core):
        full = (own, mate) if core == 0 else (mate, own)
        stores = (
            (ONE_CHIP, by_side(core, True, (w2_r, 0), (w2_x, 0))),
            (TWO_CHIPS, by_side(core, True, (w4_r, 0), (parts_x, 0))),
            (THREE_CHIPS, by_side(core, True, (w6_r, 0), (parts_x, TWO_BLOCKS * B))),
        )

        def block(m, slot):
            if 10 <= m <= 13:
                return full[(m - 10) // 2][rows_of(((m - 10) % 2) * SLOTS + slot, G_OFFSET), :]
            side = 0 if m < 10 else 1
            t = 10 - m if m < 10 else m - 13
            at = slot - t if side == 0 else slot
            ts, sides = stores[(t - 1) // 4]
            ref, base = sides[side]
            return ref[rows_of(at + place_in(ts, t), base), :]

        for pair in range(core, core + 6):
            for e in range(2):
                cols = pl.ds(e * B, B)
                for hole in ((0, 12, 13), (0, 1, 13))[e]:
                    gk[pair, pl.ds(hole * B, B), cols] = zero
                j = 2 * pair + e
                for m in range(j, j + 11):
                    gk[pair, pl.ds((m - 2 * pair + 1) * B, B), cols] = block(m, j - m + 10)

    for core in range(2):
        pl.when(p == core)(functools.partial(assemble, core))

    for r in range(2):
        lhs[pl.ds(r * B, B), pl.ds((11 if r == 0 else 0) * B, B)] = zero
        for slot in range(SLOTS):
            lhs[pl.ds(r * B, B), pl.ds((slot + r) * B, B)] = own[rows_of(r * SLOTS + slot), :]

    def tile(delta, j):
        k = j + delta
        count = (12 - 2 * abs(delta)) * B
        left = pk_ref[k + p, :, pl.ds(max(0, -delta) * 2 * B, count)]
        right = gk[j + p, pl.ds((max(0, delta) * 2 + 1) * B, count), :]
        found = jnp.dot(left, right, preferred_element_type=F32)
        found = found * mask_tile(t_ref, 2 * (k + p), 2 * (j + p), 2)
        given = gk[j + p, pl.ds((2 * delta + 6) * B, 256), :].astype(F32)
        gb[pl.ds(pl.multiple_of(k * 256, 256), 256), pl.ds(pl.multiple_of(j * 256, 256), 256)] = (
            3.0 * given - 2.0 * found
        ).astype(BF16)

    tile_loop(core_ref, tile)

    def finish(j):
        low, count = span(2 * j)
        cols = pl.ds(low * B, count * B)
        right = pk_ref[j + p, :, pl.ds((low + 5 - 2 * j) * B, count * B)]
        total = lax.dot_general(gb[pl.ds(5 * B, 256), cols], right, NT, preferred_element_type=F32)
        total += jnp.dot(
            lhs[:, cols], gb[pl.ds(low * B, count * B), pl.ds(j * 256, 256)],
            preferred_element_type=F32,
        )
        total -= 2.0 * third_s[:, pl.ds(j * 256, 256)]
        for r in range(2):
            for e in range(2):
                slot = 2 * j + e - r
                if 0 <= slot < SLOTS:
                    keep = s_ref[r, slot].astype(F32)
                    grad_ref[r, slot] = total[r * B : r * B + B, e * B : e * B + B] * keep

    def leave(j):
        ends = ((0, 2 * j, min(2 * j + 2, SLOTS)), (1, max(0, 2 * j - 1), 2 * j + 1))
        places = [(r, pl.ds(low, high - low)) for r, low, high in ends]
        return [
            pltpu.make_async_copy(grad_ref.at[at], grad_any.at[at], sems.at[2 * j + at[0]])
            for at in places
        ]

    for j in range(6):
        in_block(core_ref, functools.partial(finish, j))
        for copy in leave(j):
            copy.start()
    for j in range(6):
        for copy in leave(j):
            copy.wait()


SMEM = pl.BlockSpec(memory_space=pltpu.SMEM)
VMEM = pl.BlockSpec(memory_space=pltpu.VMEM)
HBM = pl.BlockSpec(memory_space=pltpu.HBM)


def flat(blocks, extra=0):
    return jax.ShapeDtypeStruct((blocks * B + extra, B), BF16)


def on_device(density, cotangent, s_mask, t_mask):
    devices = lax.axis_size(AXES)
    core = (lax.axis_index(AXES) % 2).astype(jnp.int32).reshape(1)
    swap = [(i, i ^ 1) for i in range(devices)]

    def send(message, hop, near=True):
        return lax.ppermute(message, AXES, route(hop, near, devices))

    def to_mate(*messages):
        return lax.ppermute(jnp.concatenate(messages, axis=0), AXES, swap)

    params = pltpu.CompilerParams(vmem_limit_bytes=30 * 1024 * 1024)
    n2, f2, n4, own, w6 = pl.pallas_call(
        pack_own,
        in_specs=[SMEM, HBM, HBM, HBM, HBM],
        out_specs=[VMEM] * 5,
        out_shape=[
            flat(13, MASK_ROWS), flat(12, MASK_ROWS), flat(6, MASK_ROWS), flat(44, MASK_ROWS),
            flat(THREE_BLOCKS),
        ],
        scratch_shapes=[
            pltpu.VMEM(density.shape, BF16), pltpu.VMEM(cotangent.shape, BF16),
            pltpu.SMEM((2, SLOTS), jnp.int32), pltpu.SMEM((2, SLOTS), jnp.int32),
            pltpu.SemaphoreType.DMA((4,)),
        ],
        compiler_params=pltpu.CompilerParams(vmem_limit_bytes=62 * 1024 * 1024),
        name="pack_own",
    )(core, s_mask, t_mask, density, cotangent)
    n2_r = send(n2, 2)
    f2_r = send(f2, 2, near=False)
    n4_r = send(n4, 4)
    mate = to_mate(own)
    w2, w4 = pl.pallas_call(
        pack_chip,
        in_specs=[SMEM, VMEM, VMEM],
        out_specs=[VMEM] * 2,
        out_shape=[flat(ONE_BLOCKS), flat(TWO_BLOCKS)],
        compiler_params=params,
        name="pack_chip",
    )(core, own, mate)
    w6_r = send(w6, 6)
    f2_r, w6_r, w2 = lax.optimization_barrier((f2_r, w6_r, w2))
    w2_r = send(w2, 2)
    w4_r = send(w4, 4)
    p_parts = to_mate(n2_r, f2_r, n4_r)

    purified, third, pk, t_all = pl.pallas_call(
        square_kernel,
        in_specs=[SMEM] + [VMEM] * 6,
        out_specs=[VMEM] * 4,
        out_shape=[
            jax.ShapeDtypeStruct((2, SLOTS, B, B), F32),
            jax.ShapeDtypeStruct((256, 1536), F32),
            jax.ShapeDtypeStruct((7, 256, 1536), BF16),
            jax.ShapeDtypeStruct((14 * 16, B), F32),
        ],
        scratch_shapes=[pltpu.VMEM((1536, 1536), BF16), pltpu.VMEM((512, 1536), BF16)],
        cost_estimate=pl.CostEstimate(flops=10**6, bytes_accessed=10**4, transcendentals=0),
        compiler_params=params,
        name="square",
    )(core, own, mate, n2_r, f2_r, n4_r, p_parts)

    w2_r, w4_g, w6_r, t_all = lax.optimization_barrier((w2_r, w4_r, w6_r, t_all))
    g_parts = to_mate(w4_g, w6_r)
    w2_x = to_mate(w2_r)

    gradient = pl.pallas_call(
        gradient_kernel,
        in_specs=[SMEM, SMEM] + [VMEM] * 10,
        out_specs=HBM,
        out_shape=jax.ShapeDtypeStruct((2, SLOTS, B, B), F32),
        scratch_shapes=[
            pltpu.VMEM((7, 14 * B, 256), BF16), pltpu.VMEM((1536, 1536), BF16),
            pltpu.VMEM((256, 1536), BF16), pltpu.VMEM((2, SLOTS, B, B), F32),
            pltpu.SemaphoreType.DMA((12,)),
        ],
        cost_estimate=pl.CostEstimate(flops=7 * 10**9, bytes_accessed=16 * 10**6, transcendentals=0),
        compiler_params=params,
        name="gradient",
    )(core, s_mask, own, mate, w2_r, w2_x, w4_g, w6_r, g_parts, pk, third, t_all)
    return (purified, gradient)


def solution(mesh):
    band = P(AXES, None, None, None)
    in_specs = (band, band, P(AXES, None), P(AXES, None))
    return jax.shard_map(
        on_device, mesh=mesh, in_specs=in_specs, out_specs=(band, band), check_vma=False
    )
```
